32 devices in a mesh: dp: 16 (over z, y, x), tensor: 2 (over core).
Axes of the slice: x: 2, y: 2, z: 4, core: 2. Of those that a mesh axis runs over, the one named last changes fastest.
Arguments:
- tokens: bfloat16 [16384, 768], P(('dp', 'tensor')), may hold values from -6 to 6
- lengths: int32 [16], P('dp'), may hold values from 1 to 1024, 10240 in all
- qkv_weight: bfloat16 [3, 768, 768], P(None, 'dp', 'tensor'), may hold values from -0.21875 to 0.21875
- qv_bias: float32 [2, 768], P(None, 'tensor'), may hold values from -3 to 3
- out_weight: bfloat16 [768, 768], P('tensor', 'dp'), may hold values from -0.875 to 0.875
- out_bias: float32 [768], replicated, may hold values from -3 to 3
- up_weight: bfloat16 [768, 3072], P('dp', 'tensor'), may hold values from -0.21875 to 0.21875
- up_bias: float32 [3072], P('tensor'), may hold values from -3 to 3
- down_weight: bfloat16 [3072, 768], P('tensor', 'dp'), may hold values from -0.109375 to 0.109375
- down_bias: float32 [768], replicated, may hold values from -3 to 3
- norm1_gain: float32 [768], replicated, may hold values from 0.5 to 1.5
- norm1_shift: float32 [768], replicated, may hold values from -3 to 3
- norm2_gain: float32 [768], replicated, may hold values from 0.5 to 1.5
- norm2_shift: float32 [768], replicated, may hold values from -3 to 3
- cotangent: bfloat16 [16384, 768], P(('dp', 'tensor')), may hold values from -6 to 6
Outputs:
- layer_output: bfloat16 [16384, 768], P(('dp', 'tensor'))
- input_grad: bfloat16 [16384, 768], P(('dp', 'tensor'))
- grad_qkv_weight: float32 [3, 768, 768], P(None, 'dp', 'tensor')
- grad_qv_bias: float32 [2, 768], P(None, 'tensor')
- grad_out_weight: float32 [768, 768], P('tensor', 'dp')
- grad_out_bias: float32 [768], replicated
- grad_up_weight: float32 [768, 3072], P('dp', 'tensor')
- grad_up_bias: float32 [3072], P('tensor')
- grad_down_weight: float32 [3072, 768], P('tensor', 'dp')
- grad_down_bias: float32 [768], replicated
- grad_norm1_gain: float32 [768], replicated
- grad_norm1_shift: float32 [768], replicated
- grad_norm2_gain: float32 [768], replicated
- grad_norm2_shift: float32 [768], replicated
The draws below stay inside these ranges and needn't reach their ends.
Inputs may be any that keep to these rules, and one draw needn't show every extreme that they name: lengths[s] is the count of real tokens of sequence s; some sequence has 1024.
All inputs are finite; a program needn't handle non-finite values. No bound on the sum of `lengths` on one device may be relied on, other than what follows from the above.
Results may differ from the reference program's by a relative error of at most 0.017.
Values may be sent and summed in bfloat16 or wider, within the bound.
A program may use at most 192 MiB of HBM per device.

```python
import math
import jax
import jax.numpy as jnp
import numpy as np
from jax import lax

D = 768
HEADS = 12
HEAD_DIM = 64
FF = 3072
LENGTH = 1024
SEQS = 16
TOKENS = 16384


def block_scale(rng, dims, split, least, largest):
    loudness, own = 1.0, jax.random.fold_in(rng, 6)
    for position, blocks in split:
        draws = jnp.exp(jax.random.uniform(jax.random.fold_in(own, position), (blocks,), jnp.float32, least / len(split), largest / len(split)))
        loudness = loudness * jnp.repeat(draws, dims[position] // blocks).reshape([-1 if axis == position else 1 for axis in range(len(dims))])
    return loudness


def length_profile(count, total, reach, skew):
    loads = [(1 << 20) // math.isqrt(rank ** skew) + 1 for rank in range(2, count + 1)]
    spare, holding = total - reach - (count - 1), [1] * (count - 1)
    while spare > 0:
        free = [i for i in range(count - 1) if holding[i] < reach]
        pool, remaining = sum([loads[i] for i in free]), spare
        for i in free:
            extra = min(reach - holding[i], max(1, remaining * loads[i] // pool), spare)
            holding[i] = holding[i] + extra
            spare = spare - extra
    return np.array([reach] + holding)


def uneven_parts(key, number_of, total, limit, skew):
    if number_of == 2:
        one = jax.random.randint(key, (), max(1, total - limit), min(limit, total - 1) + 1)
        return jnp.stack([one, total - one])
    tallies = jnp.asarray(length_profile(number_of, total, limit, skew), jnp.int32)
    pairs = (number_of - 1) // 2
    donor, taker = tallies[1:1 + 2 * pairs:2], tallies[2:2 + 2 * pairs:2]
    margin = jnp.minimum(donor - 1, limit - taker)
    passed = jax.random.randint(jax.random.fold_in(key, 1), (pairs,), 0, 1 << 20) % (margin + 1)
    tallies = tallies.at[1:1 + 2 * pairs:2].set(donor - passed).at[2:2 + 2 * pairs:2].set(taker + passed)
    return tallies[jax.random.permutation(jax.random.fold_in(key, 2), number_of)]


def bell_draw(key, dims, deviation, limit, shards=(), held_as=jnp.bfloat16):
    level = block_scale(key, dims, shards, -0.22, 0.18) if shards else 1.0
    result = jax.random.normal(key, dims, jnp.float32) * deviation * level
    return jnp.minimum(jnp.maximum(result, -limit), limit).astype(held_as)


def setup_inputs(seed: int = 0) -> dict:
    key_list = jax.random.split(jax.random.key(seed), 16)
    tokens = bell_draw(key_list[0], (TOKENS, D), 1.0, 6.0, ((0, 32),))
    lengths = uneven_parts(key_list[1], SEQS, SEQS * LENGTH * 5 // 8, LENGTH, 2).astype(jnp.int32)
    qkv_weight = bell_draw(key_list[2], (3, D, D), D ** -0.5, 0.21875, ((1, 16), (2, 2)))
    qv_bias = bell_draw(key_list[3], (2, D), 0.5, 3.0, ((1, 2),), jnp.float32)
    out_weight = bell_draw(key_list[4], (D, D), (D // 16) ** -0.5, 0.875, ((0, 2), (1, 16)))
    out_bias = bell_draw(key_list[5], (D,), 0.5, 3.0, (), jnp.float32)
    up_weight = bell_draw(key_list[6], (D, FF), D ** -0.5, 0.21875, ((0, 16), (1, 2)))
    up_bias = bell_draw(key_list[7], (FF,), 0.5, 3.0, ((0, 2),), jnp.float32)
    down_weight = bell_draw(key_list[8], (FF, D), FF ** -0.5, 0.109375, ((0, 2), (1, 16)))
    down_bias = bell_draw(key_list[9], (D,), 0.5, 3.0, (), jnp.float32)
    norm1_gain = jnp.clip(1.0 + 0.1 * jax.random.normal(key_list[10], (D,), jnp.float32), 0.5, 1.5)
    norm1_shift = bell_draw(key_list[11], (D,), 0.5, 3.0, (), jnp.float32)
    norm2_gain = jnp.clip(1.0 + 0.1 * jax.random.normal(key_list[12], (D,), jnp.float32), 0.5, 1.5)
    norm2_shift = bell_draw(key_list[13], (D,), 0.5, 3.0, (), jnp.float32)
    cotangent = bell_draw(key_list[14], (TOKENS, D), 1.0, 6.0, ((0, 32),))
    return dict(tokens=tokens, lengths=lengths, qkv_weight=qkv_weight, qv_bias=qv_bias, out_weight=out_weight, out_bias=out_bias, up_weight=up_weight, up_bias=up_bias, down_weight=down_weight, down_bias=down_bias, norm1_gain=norm1_gain, norm1_shift=norm1_shift, norm2_gain=norm2_gain, norm2_shift=norm2_shift, cotangent=cotangent)


EPSILON = 1e-05
NEGATIVE = -1e+30

@jax.custom_vjp
def low(v):
    return lax.optimization_barrier(v.astype(jnp.bfloat16)).astype(jnp.float32)

@jax.custom_vjp
def low_back(v):
    return v

def low_keep(v):
    return (low(v), None)

def low_pass(kept, grad):
    return (grad,)

def back_keep(v):
    return (v, None)

def back_low(kept, grad):
    return (low(grad),)
low.defvjp(low_keep, low_pass)
low_back.defvjp(back_keep, back_low)

def layer_norm(values, norm_gain, norm_shift):
    center = values - lax.optimization_barrier(jnp.mean(values, axis=-1, keepdims=True))
    spread = lax.optimization_barrier(jnp.mean(center * center, axis=-1, keepdims=True))
    return center * lax.rsqrt(spread + EPSILON) * norm_gain + norm_shift

def product(left, right):
    return jnp.dot(left, right, precision=lax.Precision.HIGHEST)

def attend_one(packed):
    queries, key_rows, value_rows, length = packed
    scaling = HEAD_DIM ** (-0.5)
    query_heads = queries.reshape(LENGTH, HEADS, HEAD_DIM)
    key_heads = key_rows.reshape(LENGTH, HEADS, HEAD_DIM)
    value_heads = value_rows.reshape(LENGTH, HEADS, HEAD_DIM)
    scores = jnp.einsum('qhd,khd->hqk', query_heads, key_heads, precision=lax.Precision.HIGHEST) * scaling
    scores = low_back(scores)
    usable = jnp.arange(LENGTH) < length
    scores = jnp.where(usable[None, None, :], scores, NEGATIVE)
    weights = low(jax.nn.softmax(scores, axis=-1))
    context = jnp.einsum('hqk,khd->qhd', weights, value_heads, precision=lax.Precision.HIGHEST)
    return context.reshape(LENGTH, HEADS * HEAD_DIM)

def reference(tokens, lengths, qkv_weight, qv_bias, out_weight, out_bias, up_weight, up_bias, down_weight, down_bias, norm1_gain, norm1_shift, norm2_gain, norm2_shift, cotangent):

    def forward_layer(inputs, w_qkv, b_qv, w_out, b_out, w_up, b_up, w_down, b_down, gain_one, shift_one, gain_two, shift_two):
        queries = low_back(low(product(inputs, w_qkv[0]) + b_qv[0]))
        key_rows = low_back(low(product(inputs, w_qkv[1])))
        value_rows = low_back(low(product(inputs, w_qkv[2]) + b_qv[1]))
        context = lax.map(jax.checkpoint(attend_one), (queries.reshape(SEQS, LENGTH, D), key_rows.reshape(SEQS, LENGTH, D), value_rows.reshape(SEQS, LENGTH, D), lengths))
        context = low_back(low(context.reshape(TOKENS, D)))
        attn = low_back(product(context, w_out) + b_out)
        hidden = layer_norm(inputs + attn, gain_one, shift_one)
        upper = low_back(product(low(hidden), w_up) + b_up)
        active = low(jax.nn.gelu(upper, approximate=False))
        ffn_out = low_back(product(active, w_down) + b_down)
        return layer_norm(hidden + ffn_out, gain_two, shift_two)
    primals = (tokens.astype(jnp.float32), qkv_weight.astype(jnp.float32), qv_bias, out_weight.astype(jnp.float32), out_bias, up_weight.astype(jnp.float32), up_bias, down_weight.astype(jnp.float32), down_bias, norm1_gain, norm1_shift, norm2_gain, norm2_shift)
    output, pullback = jax.vjp(forward_layer, *primals)
    gradients = pullback(cotangent.astype(jnp.float32))
    return (output.astype(jnp.bfloat16), gradients[0].astype(jnp.bfloat16), gradients[1], gradients[2], gradients[3], gradients[4], gradients[5], gradients[6], gradients[7], gradients[8], gradients[9], gradients[10], gradients[11], gradients[12])
```

```python
import jax
import jax.numpy as jnp
from jax import lax
from jax.sharding import PartitionSpec as P

HEAD_DIM = 64
LENGTH = 1024


EPSILON = 1e-05
NEGATIVE = -1e30


def layer_norm(values, norm_gain, norm_shift):
    center = values - jnp.mean(values, axis=-1, keepdims=True)
    spread = jnp.mean(center * center, axis=-1, keepdims=True)
    return center * lax.rsqrt(spread + EPSILON) * norm_gain + norm_shift


def gelu_exact(values):
    return jax.nn.gelu(values, approximate=False)


def matmul(left, right):
    return jnp.dot(left, right, preferred_element_type=jnp.float32)


def contract_rows(left, right):
    return lax.dot_general(
        left, right, (((0,), (0,)), ((), ())), preferred_element_type=jnp.float32
    )


def contract_cols(left, right):
    return lax.dot_general(
        left, right, (((1,), (1,)), ((), ())), preferred_element_type=jnp.float32
    )


def bit_orders(count):
    bits = list(range(count.bit_length() - 1))
    head, tail = bits[:3], bits[3:]
    return [head[turn:] + head[:turn] + tail for turn in range(len(head))]


def swap_bit(values, bit):
    count = lax.axis_size("dp")
    return lax.ppermute(values, "dp", [(i, i ^ (1 << bit)) for i in range(count)])


def swap_core(values):
    return lax.ppermute(values, "tensor", [(0, 1), (1, 0)])


def gather_rows(values, order):
    count = lax.axis_size("dp")
    nbits = count.bit_length() - 1
    me = lax.axis_index("dp")
    rows, cols = values.shape
    held = values.reshape((1,) * nbits + (rows, cols))
    for bit in reversed(order):
        axis = nbits - 1 - bit
        theirs = swap_bit(held, bit)
        first = (me >> bit) % 2 == 0
        held = jnp.concatenate(
            [jnp.where(first, held, theirs), jnp.where(first, theirs, held)], axis=axis
        )
    return held.reshape(count * rows, cols)


def scatter_rows(values, order):
    count = lax.axis_size("dp")
    nbits = count.bit_length() - 1
    me = lax.axis_index("dp")
    rows, cols = values.shape
    held = values.reshape((2,) * nbits + (rows // count, cols))
    for bit in order:
        axis = nbits - 1 - bit
        mine = (me >> bit) % 2
        sent = lax.dynamic_slice_in_dim(held, 1 - mine, 1, axis).astype(jnp.bfloat16)
        kept = lax.dynamic_slice_in_dim(held, mine, 1, axis)
        held = kept + swap_bit(sent, bit).astype(jnp.float32)
    return held.reshape(rows // count, cols)


def sum_small(values):
    for bit in range(lax.axis_size("dp").bit_length() - 1):
        values = values + swap_bit(values, bit)
    return values


def both(values):
    return jnp.concatenate([values, swap_core(values)], axis=0)


def sum_own(values):
    half = values.shape[0] // 2
    return values[:half] + swap_core(values[half:].astype(jnp.bfloat16)).astype(jnp.float32)


def per_device(
    tokens,
    lengths,
    qkv_weight,
    qv_bias,
    out_weight,
    out_bias,
    up_weight,
    up_bias,
    down_weight,
    down_bias,
    norm1_gain,
    norm1_shift,
    norm2_gain,
    norm2_shift,
    cotangent,
):
    tok_rows = tokens.shape[0]
    local_width = qkv_weight.shape[2]
    head_count = local_width // HEAD_DIM
    seq_count = lengths.shape[0]
    block_rows = min(512, LENGTH)
    scaling = HEAD_DIM ** (-0.5)
    positions = (jnp.arange(LENGTH) + lax.axis_index("tensor") * tok_rows) % LENGTH
    orders = bit_orders(lax.axis_size("dp"))
    turns = len(orders)
    gathered = both(tokens)

    def gather_parts(values):
        width = values.shape[1] // turns
        return jnp.concatenate(
            [
                gather_rows(values[:, p * width : (p + 1) * width], orders[p])
                for p in range(turns)
            ],
            axis=1,
        )

    def scatter_parts(values, shift=0):
        width = values.shape[1] // turns
        return jnp.concatenate(
            [
                scatter_rows(values[:, p * width : (p + 1) * width], orders[(p + shift) % turns])
                for p in range(turns)
            ],
            axis=1,
        )

    qkv_full = [gather_rows(qkv_weight[p], orders[p % turns]) for p in range(3)]
    out_full = gather_parts(out_weight.T)
    up_full = gather_parts(up_weight)
    down_full = gather_parts(down_weight.T)
    queries = (matmul(gathered, qkv_full[0]) + qv_bias[0]).astype(jnp.bfloat16)
    key_rows = matmul(gathered, qkv_full[1]).astype(jnp.bfloat16)
    value_rows = (matmul(gathered, qkv_full[2]) + qv_bias[1]).astype(jnp.bfloat16)

    def forward_seq(packed):
        seq_queries, seq_keys, seq_values, length = packed
        query_heads = seq_queries.reshape(LENGTH, head_count, HEAD_DIM)
        key_heads = seq_keys.reshape(LENGTH, head_count, HEAD_DIM)
        value_heads = seq_values.reshape(LENGTH, head_count, HEAD_DIM)
        usable = (positions < length)[None, None, :]
        context_blocks = []
        total_blocks = []
        for block_start in range(0, LENGTH, block_rows):
            block_q = query_heads[block_start : block_start + block_rows]
            scores = (
                jnp.einsum("qhd,khd->hqk", block_q, key_heads, preferred_element_type=jnp.float32)
                * scaling
            )
            scores = jnp.where(usable, scores, NEGATIVE)
            row_top = jnp.max(scores, axis=-1, keepdims=True)
            exponent = jnp.exp(scores - row_top)
            row_total = jnp.sum(exponent, axis=-1, keepdims=True)
            weights = (exponent / row_total).astype(jnp.bfloat16)
            block_context = jnp.einsum(
                "hqk,khd->qhd", weights, value_heads, preferred_element_type=jnp.float32
            )
            context_blocks.append(block_context.reshape(block_rows, local_width))
            total_blocks.append((row_top + jnp.log(row_total))[..., 0])
        return (
            jnp.concatenate(context_blocks, axis=0).astype(jnp.bfloat16),
            jnp.concatenate(total_blocks, axis=1),
        )

    shaped = (
        queries.reshape(seq_count, LENGTH, local_width),
        key_rows.reshape(seq_count, LENGTH, local_width),
        value_rows.reshape(seq_count, LENGTH, local_width),
    )
    contexts, log_totals = lax.map(forward_seq, (shaped[0], shaped[1], shaped[2], lengths))
    context_flat = contexts.reshape(seq_count * LENGTH, local_width)
    attn = sum_own(contract_cols(context_flat, out_full)) + out_bias
    first_sum = tokens.astype(jnp.float32) + attn
    hidden = layer_norm(first_sum, norm1_gain, norm1_shift)
    hidden_low = hidden.astype(jnp.bfloat16)
    hidden_all = both(hidden_low)
    upper = matmul(hidden_all, up_full) + up_bias
    active = gelu_exact(upper).astype(jnp.bfloat16)
    ffn_out = sum_own(contract_cols(active, down_full)) + down_bias
    second_sum = hidden + ffn_out
    layer_output = layer_norm(second_sum, norm2_gain, norm2_shift).astype(jnp.bfloat16)
    qkv_back, out_back, up_back, down_back = (qkv_full, out_full, up_full, down_full)
    unused_two, norm_two_back = jax.vjp(layer_norm, second_sum, norm2_gain, norm2_shift)
    grad_second, gain_two_grad, shift_two_grad = norm_two_back(cotangent.astype(jnp.float32))
    grad_ffn = grad_second.astype(jnp.bfloat16)
    down_bias_grad = jnp.sum(grad_ffn.astype(jnp.float32), axis=0)
    grad_ffn_all = both(grad_ffn)
    down_weight_grad = contract_rows(grad_ffn_all, active)
    grad_active = matmul(grad_ffn_all, down_back)
    unused_gelu, gelu_back = jax.vjp(gelu_exact, upper)
    grad_upper = gelu_back(grad_active)[0].astype(jnp.bfloat16)
    up_bias_grad = jnp.sum(grad_upper.astype(jnp.float32), axis=0)
    up_weight_grad = contract_rows(hidden_all, grad_upper)
    grad_hidden = grad_second + sum_own(contract_cols(grad_upper, up_back))
    unused_one, norm_one_back = jax.vjp(layer_norm, first_sum, norm1_gain, norm1_shift)
    grad_first, gain_one_grad, shift_one_grad = norm_one_back(grad_hidden)
    grad_attn = grad_first.astype(jnp.bfloat16)
    out_bias_grad = jnp.sum(grad_attn.astype(jnp.float32), axis=0)
    grad_attn_all = both(grad_attn)
    out_weight_grad = contract_rows(grad_attn_all, context_flat)
    grad_context = matmul(grad_attn_all, out_back).astype(jnp.bfloat16)

    def backward_seq(packed):
        seq_queries, seq_keys, seq_values, length, seq_grad, seq_totals = packed
        query_heads = seq_queries.reshape(LENGTH, head_count, HEAD_DIM)
        key_heads = seq_keys.reshape(LENGTH, head_count, HEAD_DIM)
        value_heads = seq_values.reshape(LENGTH, head_count, HEAD_DIM)
        usable = (positions < length)[None, None, :]
        key_grad = jnp.zeros((LENGTH, head_count, HEAD_DIM), jnp.float32)
        value_grad = jnp.zeros((LENGTH, head_count, HEAD_DIM), jnp.float32)
        query_blocks = []
        for block_start in range(0, LENGTH, block_rows):
            block_q = query_heads[block_start : block_start + block_rows]
            block_grad = seq_grad[block_start : block_start + block_rows].reshape(
                block_rows, head_count, HEAD_DIM
            )
            scores = (
                jnp.einsum("qhd,khd->hqk", block_q, key_heads, preferred_element_type=jnp.float32)
                * scaling
            )
            scores = jnp.where(usable, scores, NEGATIVE)
            chances = jnp.exp(scores - seq_totals[:, block_start : block_start + block_rows, None])
            weights = chances.astype(jnp.bfloat16)
            value_grad = value_grad + jnp.einsum(
                "hqk,qhd->khd", weights, block_grad, preferred_element_type=jnp.float32
            )
            grad_weights = jnp.einsum(
                "qhd,khd->hqk", block_grad, value_heads, preferred_element_type=jnp.float32
            )
            inner_sum = jnp.sum(grad_weights * chances, axis=-1, keepdims=True)
            grad_scores = (chances * (grad_weights - inner_sum)).astype(jnp.bfloat16)
            block_query_grad = (
                jnp.einsum(
                    "hqk,khd->qhd", grad_scores, key_heads, preferred_element_type=jnp.float32
                )
                * scaling
            )
            query_blocks.append(block_query_grad.reshape(block_rows, local_width))
            key_grad = (
                key_grad
                + jnp.einsum(
                    "hqk,qhd->khd", grad_scores, block_q, preferred_element_type=jnp.float32
                )
                * scaling
            )
        query_grad = jnp.concatenate(query_blocks, axis=0).astype(jnp.bfloat16)
        return (
            query_grad,
            key_grad.reshape(LENGTH, local_width).astype(jnp.bfloat16),
            value_grad.reshape(LENGTH, local_width).astype(jnp.bfloat16),
        )

    grad_shaped = grad_context.reshape(seq_count, LENGTH, local_width)
    query_grads, key_grads, value_grads = lax.map(
        backward_seq, (shaped[0], shaped[1], shaped[2], lengths, grad_shaped, log_totals)
    )
    query_grads = query_grads.reshape(seq_count * LENGTH, local_width)
    key_grads = key_grads.reshape(seq_count * LENGTH, local_width)
    value_grads = value_grads.reshape(seq_count * LENGTH, local_width)
    qv_bias_grad = jnp.stack(
        [
            jnp.sum(query_grads.astype(jnp.float32), axis=0),
            jnp.sum(value_grads.astype(jnp.float32), axis=0),
        ]
    )
    qkv_grad_own = jnp.stack(
        [
            scatter_rows(contract_rows(gathered, grads), orders[p % turns])
            for p, grads in enumerate((query_grads, key_grads, value_grads))
        ]
    )
    input_grad = (
        grad_first
        + sum_own(
            contract_cols(query_grads, qkv_back[0])
            + contract_cols(key_grads, qkv_back[1])
            + contract_cols(value_grads, qkv_back[2])
        )
    ).astype(jnp.bfloat16)
    out_grad_own = scatter_parts(out_weight_grad).T
    up_grad_own = scatter_parts(up_weight_grad)
    down_grad_own = scatter_parts(down_weight_grad).T
    whole = jnp.stack(
        [
            out_bias_grad,
            down_bias_grad,
            gain_one_grad,
            shift_one_grad,
            gain_two_grad,
            shift_two_grad,
        ]
    )
    split = jnp.concatenate([qv_bias_grad.reshape(-1), up_bias_grad])
    (
        out_bias_total,
        down_bias_total,
        gain_one_total,
        shift_one_total,
        gain_two_total,
        shift_two_total,
    ) = sum_small(whole + swap_core(whole))
    split_total = sum_small(split)
    qv_bias_total = split_total[: 2 * local_width].reshape(2, local_width)
    up_bias_total = split_total[2 * local_width :]
    return (
        layer_output,
        input_grad,
        qkv_grad_own,
        qv_bias_total,
        out_grad_own,
        out_bias_total,
        up_grad_own,
        up_bias_total,
        down_grad_own,
        down_bias_total,
        gain_one_total,
        shift_one_total,
        gain_two_total,
        shift_two_total,
    )


def solution(mesh):
    return jax.shard_map(
        per_device,
        mesh=mesh,
        in_specs=(
            P(("dp", "tensor"), None),
            P("dp"),
            P(None, "dp", "tensor"),
            P(None, "tensor"),
            P("tensor", "dp"),
            P(),
            P("dp", "tensor"),
            P("tensor"),
            P("tensor", "dp"),
            P(),
            P(),
            P(),
            P(),
            P(),
            P(("dp", "tensor"), None),
        ),
        out_specs=(
            P(("dp", "tensor"), None),
            P(("dp", "tensor"), None),
            P(None, "dp", "tensor"),
            P(None, "tensor"),
            P("tensor", "dp"),
            P(),
            P("dp", "tensor"),
            P("tensor"),
            P("tensor", "dp"),
            P(),
            P(),
            P(),
            P(),
            P(),
        ),
        check_vma=False,
    )
```

```python
import jax
import jax.numpy as jnp
from jax import lax
from jax.sharding import PartitionSpec as P

HEAD_DIM = 64
LENGTH = 1024


EPSILON = 1e-05
NEGATIVE = -1e30


def layer_norm(values, norm_gain, norm_shift):
    center = values - jnp.mean(values, axis=-1, keepdims=True)
    spread = jnp.mean(center * center, axis=-1, keepdims=True)
    return center * lax.rsqrt(spread + EPSILON) * norm_gain + norm_shift


def gelu_exact(values):
    return jax.nn.gelu(values, approximate=False)


def matmul(left, right):
    return jnp.dot(left, right, preferred_element_type=jnp.float32)


def contract_rows(left, right):
    return lax.dot_general(
        left, right, (((0,), (0,)), ((), ())), preferred_element_type=jnp.float32
    )


def contract_cols(left, right):
    return lax.dot_general(
        left, right, (((1,), (1,)), ((), ())), preferred_element_type=jnp.float32
    )


def bit_orders(count):
    bits = list(range(count.bit_length() - 1))
    head, tail = bits[:3], bits[3:]
    return [head[turn:] + head[:turn] + tail for turn in range(len(head))]


def swap_bit(values, bit):
    count = lax.axis_size("dp")
    return lax.ppermute(values, "dp", [(i, i ^ (1 << bit)) for i in range(count)])


def swap_core(values):
    return lax.ppermute(values, "tensor", [(0, 1), (1, 0)])


def gather_rows(values, order):
    count = lax.axis_size("dp")
    nbits = count.bit_length() - 1
    me = lax.axis_index("dp")
    rows, cols = values.shape
    held = values.reshape((1,) * nbits + (rows, cols))
    for bit in reversed(order):
        axis = nbits - 1 - bit
        theirs = swap_bit(held, bit)
        first = (me >> bit) % 2 == 0
        held = jnp.concatenate(
            [jnp.where(first, held, theirs), jnp.where(first, theirs, held)], axis=axis
        )
    return held.reshape(count * rows, cols)


def scatter_open(values):
    count = lax.axis_size("dp")
    rows, cols = values.shape
    return values.reshape((2,) * (count.bit_length() - 1) + (rows // count, cols))


def scatter_step(held, bit):
    axis = lax.axis_size("dp").bit_length() - 2 - bit
    mine = (lax.axis_index("dp") >> bit) % 2
    sent = lax.dynamic_slice_in_dim(held, 1 - mine, 1, axis).astype(jnp.bfloat16)
    kept = lax.dynamic_slice_in_dim(held, mine, 1, axis)
    return kept + swap_bit(sent, bit).astype(jnp.float32)


def scatter_rows(values, order):
    held = scatter_open(values)
    for bit in order:
        held = scatter_step(held, bit)
    return held.reshape(held.shape[-2:])


def sum_small(values):
    for bit in range(lax.axis_size("dp").bit_length() - 1):
        values = values + swap_bit(values, bit)
    return values


def both(values):
    return jnp.concatenate([values, swap_core(values)], axis=0)


def sum_own(values):
    half = values.shape[0] // 2
    return values[:half] + swap_core(values[half:].astype(jnp.bfloat16)).astype(jnp.float32)


def per_device(
    tokens,
    lengths,
    qkv_weight,
    qv_bias,
    out_weight,
    out_bias,
    up_weight,
    up_bias,
    down_weight,
    down_bias,
    norm1_gain,
    norm1_shift,
    norm2_gain,
    norm2_shift,
    cotangent,
):
    tok_rows = tokens.shape[0]
    local_width = qkv_weight.shape[2]
    head_count = local_width // HEAD_DIM
    seq_count = lengths.shape[0]
    block_rows = min(512, LENGTH)
    scaling = HEAD_DIM ** (-0.5)
    positions = (jnp.arange(LENGTH) + lax.axis_index("tensor") * tok_rows) % LENGTH
    orders = bit_orders(lax.axis_size("dp"))
    turns = len(orders)
    gathered = both(tokens)

    def gather_parts(values):
        width = values.shape[1] // turns
        return jnp.concatenate(
            [
                gather_rows(values[:, p * width : (p + 1) * width], orders[p])
                for p in range(turns)
            ],
            axis=1,
        )

    qkv_full = [gather_rows(qkv_weight[p], orders[p % turns]) for p in range(3)]
    out_width, up_width = out_weight.shape[0], up_weight.shape[1]
    later = jnp.concatenate([out_weight.T, up_weight, down_weight.T], axis=1)
    gathered, qkv_full, later = lax.optimization_barrier((gathered, qkv_full, later))
    later_full = gather_parts(later)
    out_full = later_full[:, :out_width]
    up_full = later_full[:, out_width : out_width + up_width]
    down_full = later_full[:, out_width + up_width :]
    queries = (matmul(gathered, qkv_full[0]) + qv_bias[0]).astype(jnp.bfloat16)
    key_rows = matmul(gathered, qkv_full[1]).astype(jnp.bfloat16)
    value_rows = (matmul(gathered, qkv_full[2]) + qv_bias[1]).astype(jnp.bfloat16)

    def forward_seq(packed):
        seq_queries, seq_keys, seq_values, length = packed
        query_heads = seq_queries.reshape(LENGTH, head_count, HEAD_DIM)
        key_heads = seq_keys.reshape(LENGTH, head_count, HEAD_DIM)
        value_heads = seq_values.reshape(LENGTH, head_count, HEAD_DIM)
        usable = (positions < length)[None, None, :]
        context_blocks = []
        total_blocks = []
        for block_start in range(0, LENGTH, block_rows):
            block_q = query_heads[block_start : block_start + block_rows]
            scores = (
                jnp.einsum("qhd,khd->hqk", block_q, key_heads, preferred_element_type=jnp.float32)
                * scaling
            )
            scores = jnp.where(usable, scores, NEGATIVE)
            row_top = jnp.max(scores, axis=-1, keepdims=True)
            exponent = jnp.exp(scores - row_top)
            row_total = jnp.sum(exponent, axis=-1, keepdims=True)
            weights = (exponent / row_total).astype(jnp.bfloat16)
            block_context = jnp.einsum(
                "hqk,khd->qhd", weights, value_heads, preferred_element_type=jnp.float32
            )
            context_blocks.append(block_context.reshape(block_rows, local_width))
            total_blocks.append((row_top + jnp.log(row_total))[..., 0])
        return (
            jnp.concatenate(context_blocks, axis=0).astype(jnp.bfloat16),
            jnp.concatenate(total_blocks, axis=1),
        )

    shaped = (
        queries.reshape(seq_count, LENGTH, local_width),
        key_rows.reshape(seq_count, LENGTH, local_width),
        value_rows.reshape(seq_count, LENGTH, local_width),
    )
    contexts, log_totals = lax.map(forward_seq, (shaped[0], shaped[1], shaped[2], lengths))
    context_flat = contexts.reshape(seq_count * LENGTH, local_width)
    attn = sum_own(contract_cols(context_flat, out_full)) + out_bias
    first_sum = tokens.astype(jnp.float32) + attn
    hidden = layer_norm(first_sum, norm1_gain, norm1_shift)
    hidden_low = hidden.astype(jnp.bfloat16)
    hidden_all = both(hidden_low)
    upper = matmul(hidden_all, up_full) + up_bias
    active = gelu_exact(upper).astype(jnp.bfloat16)
    ffn_out = sum_own(contract_cols(active, down_full)) + down_bias
    second_sum = hidden + ffn_out
    layer_output = layer_norm(second_sum, norm2_gain, norm2_shift).astype(jnp.bfloat16)
    qkv_back, out_back, up_back, down_back = (qkv_full, out_full, up_full, down_full)
    unused_two, norm_two_back = jax.vjp(layer_norm, second_sum, norm2_gain, norm2_shift)
    grad_second, gain_two_grad, shift_two_grad = norm_two_back(cotangent.astype(jnp.float32))
    grad_ffn = grad_second.astype(jnp.bfloat16)
    down_bias_grad = jnp.sum(grad_ffn.astype(jnp.float32), axis=0)
    grad_ffn_all = both(grad_ffn)
    down_weight_grad = contract_rows(grad_ffn_all, active)
    grad_active = matmul(grad_ffn_all, down_back)
    unused_gelu, gelu_back = jax.vjp(gelu_exact, upper)
    grad_upper = gelu_back(grad_active)[0].astype(jnp.bfloat16)
    up_bias_grad = jnp.sum(grad_upper.astype(jnp.float32), axis=0)
    up_weight_grad = contract_rows(hidden_all, grad_upper)
    grad_hidden = grad_second + sum_own(contract_cols(grad_upper, up_back))
    unused_one, norm_one_back = jax.vjp(layer_norm, first_sum, norm1_gain, norm1_shift)
    grad_first, gain_one_grad, shift_one_grad = norm_one_back(grad_hidden)
    grad_attn = grad_first.astype(jnp.bfloat16)
    out_bias_grad = jnp.sum(grad_attn.astype(jnp.float32), axis=0)
    grad_attn_all = both(grad_attn)
    out_weight_grad = contract_rows(grad_attn_all, context_flat)
    grad_context = matmul(grad_attn_all, out_back).astype(jnp.bfloat16)
    early = jnp.concatenate([out_weight_grad, up_weight_grad, down_weight_grad], axis=1)
    part_width = early.shape[1] // turns
    held = [
        scatter_open(early[:, p * part_width : (p + 1) * part_width]) for p in range(turns)
    ]

    def early_steps(held, start, stop):
        for step in range(start, stop):
            held = [scatter_step(part, orders[p][step]) for p, part in enumerate(held)]
        return held

    whole = jnp.stack(
        [
            out_bias_grad,
            down_bias_grad,
            gain_one_grad,
            shift_one_grad,
            gain_two_grad,
            shift_two_grad,
        ]
    )
    whole_size = whole.size
    early_small = sum_small(
        jnp.concatenate([(whole + swap_core(whole)).reshape(-1), up_bias_grad]).reshape(-1, 128)
    ).reshape(-1)

    def backward_seq(packed, held):
        seq_queries, seq_keys, seq_values, length, seq_grad, seq_totals = packed
        query_heads = seq_queries.reshape(LENGTH, head_count, HEAD_DIM)
        key_heads = seq_keys.reshape(LENGTH, head_count, HEAD_DIM)
        value_heads = seq_values.reshape(LENGTH, head_count, HEAD_DIM)
        usable = (positions < length)[None, None, :]
        key_grad = jnp.zeros((LENGTH, head_count, HEAD_DIM), jnp.float32)
        value_grad = jnp.zeros((LENGTH, head_count, HEAD_DIM), jnp.float32)
        query_blocks = []
        for block_start in range(0, LENGTH, block_rows):
            block_q = query_heads[block_start : block_start + block_rows]
            block_grad = seq_grad[block_start : block_start + block_rows].reshape(
                block_rows, head_count, HEAD_DIM
            )
            if block_start:
                block_q, block_grad, key_grad, value_grad, held = lax.optimization_barrier(
                    (block_q, block_grad, key_grad, value_grad, early_steps(held, 0, 1))
                )
            scores = (
                jnp.einsum("qhd,khd->hqk", block_q, key_heads, preferred_element_type=jnp.float32)
                * scaling
            )
            scores = jnp.where(usable, scores, NEGATIVE)
            chances = jnp.exp(scores - seq_totals[:, block_start : block_start + block_rows, None])
            weights = chances.astype(jnp.bfloat16)
            value_grad = value_grad + jnp.einsum(
                "hqk,qhd->khd", weights, block_grad, preferred_element_type=jnp.float32
            )
            grad_weights = jnp.einsum(
                "qhd,khd->hqk", block_grad, value_heads, preferred_element_type=jnp.float32
            )
            inner_sum = jnp.sum(grad_weights * chances, axis=-1, keepdims=True)
            grad_scores = (chances * (grad_weights - inner_sum)).astype(jnp.bfloat16)
            block_query_grad = (
                jnp.einsum(
                    "hqk,khd->qhd", grad_scores, key_heads, preferred_element_type=jnp.float32
                )
                * scaling
            )
            query_blocks.append(block_query_grad.reshape(block_rows, local_width))
            key_grad = (
                key_grad
                + jnp.einsum(
                    "hqk,qhd->khd", grad_scores, block_q, preferred_element_type=jnp.float32
                )
                * scaling
            )
        query_grad = jnp.concatenate(query_blocks, axis=0)
        query_grad, key_grad, value_grad, held = lax.optimization_barrier(
            (query_grad, key_grad, value_grad, early_steps(held, 1, 2))
        )
        return (
            query_grad.astype(jnp.bfloat16),
            key_grad.reshape(LENGTH, local_width).astype(jnp.bfloat16),
            value_grad.reshape(LENGTH, local_width).astype(jnp.bfloat16),
            held,
        )

    query_grads, key_grads, value_grads, held = backward_seq(
        (queries, key_rows, value_rows, lengths[0], grad_context, log_totals[0]), held
    )
    early_own = jnp.concatenate(
        [part.reshape(part.shape[-2:]) for part in early_steps(held, 2, len(orders[0]))], axis=1
    )
    query_grads = query_grads.reshape(seq_count * LENGTH, local_width)
    key_grads = key_grads.reshape(seq_count * LENGTH, local_width)
    value_grads = value_grads.reshape(seq_count * LENGTH, local_width)
    qv_bias_grad = jnp.stack(
        [
            jnp.sum(query_grads.astype(jnp.float32), axis=0),
            jnp.sum(value_grads.astype(jnp.float32), axis=0),
        ]
    )
    qkv_grad_own = jnp.stack(
        [
            scatter_rows(contract_rows(gathered, grads), orders[p % turns])
            for p, grads in enumerate((query_grads, key_grads, value_grads))
        ]
    )
    input_grad = (
        grad_first
        + sum_own(
            contract_cols(query_grads, qkv_back[0])
            + contract_cols(key_grads, qkv_back[1])
            + contract_cols(value_grads, qkv_back[2])
        )
    ).astype(jnp.bfloat16)
    qv_bias_total = sum_small(qv_bias_grad)
    out_grad_own = early_own[:, :out_width].T
    up_grad_own = early_own[:, out_width : out_width + up_width]
    down_grad_own = early_own[:, out_width + up_width :].T
    (
        out_bias_total,
        down_bias_total,
        gain_one_total,
        shift_one_total,
        gain_two_total,
        shift_two_total,
    ) = early_small[:whole_size].reshape(whole.shape)
    up_bias_total = early_small[whole_size:]
    return (
        layer_output,
        input_grad,
        qkv_grad_own,
        qv_bias_total,
        out_grad_own,
        out_bias_total,
        up_grad_own,
        up_bias_total,
        down_grad_own,
        down_bias_total,
        gain_one_total,
        shift_one_total,
        gain_two_total,
        shift_two_total,
    )


def solution(mesh):
    return jax.shard_map(
        per_device,
        mesh=mesh,
        in_specs=(
            P(("dp", "tensor"), None),
            P("dp"),
            P(None, "dp", "tensor"),
            P(None, "tensor"),
            P("tensor", "dp"),
            P(),
            P("dp", "tensor"),
            P("tensor"),
            P("tensor", "dp"),
            P(),
            P(),
            P(),
            P(),
            P(),
            P(("dp", "tensor"), None),
        ),
        out_specs=(
            P(("dp", "tensor"), None),
            P(("dp", "tensor"), None),
            P(None, "dp", "tensor"),
            P(None, "tensor"),
            P("tensor", "dp"),
            P(),
            P("dp", "tensor"),
            P("tensor"),
            P("tensor", "dp"),
            P(),
            P(),
            P(),
            P(),
            P(),
        ),
        check_vma=False,
    )
```

```python
import jax
import jax.numpy as jnp
from jax import lax
from jax.sharding import PartitionSpec as P

HEAD_DIM = 64
LENGTH = 1024


EPSILON = 1e-05
NEGATIVE = -1e30


def layer_norm(values, norm_gain, norm_shift):
    center = values - jnp.mean(values, axis=-1, keepdims=True)
    spread = jnp.mean(center * center, axis=-1, keepdims=True)
    return center * lax.rsqrt(spread + EPSILON) * norm_gain + norm_shift


def gelu_exact(values):
    return jax.nn.gelu(values, approximate=False)


def matmul(left, right):
    return jnp.dot(left, right, preferred_element_type=jnp.float32)


def contract_rows(left, right):
    return lax.dot_general(
        left, right, (((0,), (0,)), ((), ())), preferred_element_type=jnp.float32
    )


def contract_cols(left, right):
    return lax.dot_general(
        left, right, (((1,), (1,)), ((), ())), preferred_element_type=jnp.float32
    )


def bit_orders(count):
    bits = list(range(count.bit_length() - 1))
    head, tail = bits[:3], bits[3:]
    return [head[turn:] + head[:turn] + tail for turn in range(len(head))]


def swap_bit(values, bit):
    count = lax.axis_size("dp")
    return lax.ppermute(values, "dp", [(i, i ^ (1 << bit)) for i in range(count)])


def swap_core(values):
    return lax.ppermute(values, "tensor", [(0, 1), (1, 0)])


def gather_rows(values, order):
    count = lax.axis_size("dp")
    nbits = count.bit_length() - 1
    me = lax.axis_index("dp")
    rows, cols = values.shape
    held = values.reshape((1,) * nbits + (rows, cols))
    for bit in reversed(order):
        axis = nbits - 1 - bit
        theirs = swap_bit(held, bit)
        first = (me >> bit) % 2 == 0
        held = jnp.concatenate(
            [jnp.where(first, held, theirs), jnp.where(first, theirs, held)], axis=axis
        )
    return held.reshape(count * rows, cols)


def scatter_open(values):
    count = lax.axis_size("dp")
    rows, cols = values.shape
    return values.reshape((2,) * (count.bit_length() - 1) + (rows // count, cols))


def scatter_step(held, bit):
    axis = lax.axis_size("dp").bit_length() - 2 - bit
    mine = (lax.axis_index("dp") >> bit) % 2
    sent = lax.dynamic_slice_in_dim(held, 1 - mine, 1, axis).astype(jnp.bfloat16)
    kept = lax.dynamic_slice_in_dim(held, mine, 1, axis)
    return kept + swap_bit(sent, bit).astype(jnp.float32)


def scatter_rows(values, order):
    held = scatter_open(values)
    for bit in order:
        held = scatter_step(held, bit)
    return held.reshape(held.shape[-2:])


def sum_small(values):
    for bit in range(lax.axis_size("dp").bit_length() - 1):
        values = values + swap_bit(values, bit)
    return values


def both(values):
    return jnp.concatenate([values, swap_core(values)], axis=0)


def sum_own(values):
    half = values.shape[0] // 2
    return values[:half] + swap_core(values[half:].astype(jnp.bfloat16)).astype(jnp.float32)


def per_device(
    tokens,
    lengths,
    qkv_weight,
    qv_bias,
    out_weight,
    out_bias,
    up_weight,
    up_bias,
    down_weight,
    down_bias,
    norm1_gain,
    norm1_shift,
    norm2_gain,
    norm2_shift,
    cotangent,
):
    tok_rows = tokens.shape[0]
    local_width = qkv_weight.shape[2]
    head_count = local_width // HEAD_DIM
    seq_count = lengths.shape[0]
    block_rows = min(512, LENGTH)
    scaling = HEAD_DIM ** (-0.5)
    positions = (jnp.arange(LENGTH) + lax.axis_index("tensor") * tok_rows) % LENGTH
    orders = bit_orders(lax.axis_size("dp"))
    turns = len(orders)
    gathered = both(tokens)

    def gather_parts(values):
        width = values.shape[1] // turns
        return jnp.concatenate(
            [
                gather_rows(values[:, p * width : (p + 1) * width], orders[p])
                for p in range(turns)
            ],
            axis=1,
        )

    qkv_full = [gather_rows(qkv_weight[p], orders[p % turns]) for p in range(3)]
    out_width, up_width = out_weight.shape[0], up_weight.shape[1]
    later = jnp.concatenate([out_weight.T, up_weight, down_weight.T], axis=1)
    gathered, qkv_full, later = lax.optimization_barrier((gathered, qkv_full, later))
    later_full = gather_parts(later)
    out_full = later_full[:, :out_width]
    up_full = later_full[:, out_width : out_width + up_width]
    down_full = later_full[:, out_width + up_width :]
    queries = (matmul(gathered, qkv_full[0]) + qv_bias[0]).astype(jnp.bfloat16)
    key_rows = matmul(gathered, qkv_full[1]).astype(jnp.bfloat16)
    value_rows = (matmul(gathered, qkv_full[2]) + qv_bias[1]).astype(jnp.bfloat16)

    def forward_seq(packed):
        seq_queries, seq_keys, seq_values, length = packed
        query_heads = seq_queries.reshape(LENGTH, head_count, HEAD_DIM)
        key_heads = seq_keys.reshape(LENGTH, head_count, HEAD_DIM)
        value_heads = seq_values.reshape(LENGTH, head_count, HEAD_DIM)
        usable = (positions < length)[None, None, :]
        context_blocks = []
        total_blocks = []
        for block_start in range(0, LENGTH, block_rows):
            block_q = query_heads[block_start : block_start + block_rows]
            scores = (
                jnp.einsum("qhd,khd->hqk", block_q, key_heads, preferred_element_type=jnp.float32)
                * scaling
            )
            scores = jnp.where(usable, scores, NEGATIVE)
            row_top = jnp.max(scores, axis=-1, keepdims=True)
            exponent = jnp.exp(scores - row_top)
            row_total = jnp.sum(exponent, axis=-1, keepdims=True)
            weights = (exponent / row_total).astype(jnp.bfloat16)
            block_context = jnp.einsum(
                "hqk,khd->qhd", weights, value_heads, preferred_element_type=jnp.float32
            )
            context_blocks.append(block_context.reshape(block_rows, local_width))
            total_blocks.append((row_top + jnp.log(row_total))[..., 0])
        return (
            jnp.concatenate(context_blocks, axis=0).astype(jnp.bfloat16),
            jnp.concatenate(total_blocks, axis=1),
        )

    shaped = (
        queries.reshape(seq_count, LENGTH, local_width),
        key_rows.reshape(seq_count, LENGTH, local_width),
        value_rows.reshape(seq_count, LENGTH, local_width),
    )
    contexts, log_totals = lax.map(forward_seq, (shaped[0], shaped[1], shaped[2], lengths))
    context_flat = contexts.reshape(seq_count * LENGTH, local_width)
    attn = sum_own(contract_cols(context_flat, out_full)) + out_bias
    first_sum = tokens.astype(jnp.float32) + attn
    hidden = layer_norm(first_sum, norm1_gain, norm1_shift)
    hidden_low = hidden.astype(jnp.bfloat16)
    hidden_all = both(hidden_low)
    upper = matmul(hidden_all, up_full) + up_bias
    active = gelu_exact(upper).astype(jnp.bfloat16)
    ffn_out = sum_own(contract_cols(active, down_full)) + down_bias
    second_sum = hidden + ffn_out
    layer_output = layer_norm(second_sum, norm2_gain, norm2_shift).astype(jnp.bfloat16)
    qkv_back, out_back, up_back, down_back = (qkv_full, out_full, up_full, down_full)
    unused_two, norm_two_back = jax.vjp(layer_norm, second_sum, norm2_gain, norm2_shift)
    grad_second, gain_two_grad, shift_two_grad = norm_two_back(cotangent.astype(jnp.float32))
    grad_ffn = grad_second.astype(jnp.bfloat16)
    down_bias_grad = jnp.sum(grad_ffn.astype(jnp.float32), axis=0)
    grad_ffn_all = both(grad_ffn)
    down_weight_grad = contract_rows(grad_ffn_all, active)
    grad_active = matmul(grad_ffn_all, down_back)
    unused_gelu, gelu_back = jax.vjp(gelu_exact, upper)
    grad_upper = gelu_back(grad_active)[0].astype(jnp.bfloat16)
    up_bias_grad = jnp.sum(grad_upper.astype(jnp.float32), axis=0)
    up_weight_grad = contract_rows(hidden_all, grad_upper)
    grad_hidden = grad_second + sum_own(contract_cols(grad_upper, up_back))
    unused_one, norm_one_back = jax.vjp(layer_norm, first_sum, norm1_gain, norm1_shift)
    grad_first, gain_one_grad, shift_one_grad = norm_one_back(grad_hidden)
    grad_attn = grad_first.astype(jnp.bfloat16)
    out_bias_grad = jnp.sum(grad_attn.astype(jnp.float32), axis=0)
    grad_attn_all = both(grad_attn)
    out_weight_grad = contract_rows(grad_attn_all, context_flat)
    grad_context = matmul(grad_attn_all, out_back).astype(jnp.bfloat16)
    early = jnp.concatenate([out_weight_grad, up_weight_grad, down_weight_grad], axis=1)
    part_width = early.shape[1] // turns
    held = [
        scatter_open(early[:, p * part_width : (p + 1) * part_width]) for p in range(turns)
    ]

    def early_steps(held, start, stop):
        for step in range(start, stop):
            held = [scatter_step(part, orders[p][step]) for p, part in enumerate(held)]
        return held


    def backward_seq(packed, held):
        seq_queries, seq_keys, seq_values, length, seq_grad, seq_totals = packed
        query_heads = seq_queries.reshape(LENGTH, head_count, HEAD_DIM)
        key_heads = seq_keys.reshape(LENGTH, head_count, HEAD_DIM)
        value_heads = seq_values.reshape(LENGTH, head_count, HEAD_DIM)
        usable = (positions < length)[None, None, :]
        key_grad = jnp.zeros((LENGTH, head_count, HEAD_DIM), jnp.float32)
        value_grad = jnp.zeros((LENGTH, head_count, HEAD_DIM), jnp.float32)
        query_blocks = []
        for block_start in range(0, LENGTH, block_rows):
            block_q = query_heads[block_start : block_start + block_rows]
            block_grad = seq_grad[block_start : block_start + block_rows].reshape(
                block_rows, head_count, HEAD_DIM
            )
            if block_start:
                block_q, block_grad, key_grad, value_grad, held = lax.optimization_barrier(
                    (block_q, block_grad, key_grad, value_grad, early_steps(held, 0, 1))
                )
            scores = (
                jnp.einsum("qhd,khd->hqk", block_q, key_heads, preferred_element_type=jnp.float32)
                * scaling
            )
            scores = jnp.where(usable, scores, NEGATIVE)
            chances = jnp.exp(scores - seq_totals[:, block_start : block_start + block_rows, None])
            weights = chances.astype(jnp.bfloat16)
            value_grad = value_grad + jnp.einsum(
                "hqk,qhd->khd", weights, block_grad, preferred_element_type=jnp.float32
            )
            grad_weights = jnp.einsum(
                "qhd,khd->hqk", block_grad, value_heads, preferred_element_type=jnp.float32
            )
            inner_sum = jnp.sum(grad_weights * chances, axis=-1, keepdims=True)
            grad_scores = (chances * (grad_weights - inner_sum)).astype(jnp.bfloat16)
            block_query_grad = (
                jnp.einsum(
                    "hqk,khd->qhd", grad_scores, key_heads, preferred_element_type=jnp.float32
                )
                * scaling
            )
            query_blocks.append(block_query_grad.reshape(block_rows, local_width))
            key_grad = (
                key_grad
                + jnp.einsum(
                    "hqk,qhd->khd", grad_scores, block_q, preferred_element_type=jnp.float32
                )
                * scaling
            )
        query_grad = jnp.concatenate(query_blocks, axis=0)
        query_grad, key_grad, value_grad, held = lax.optimization_barrier(
            (query_grad, key_grad, value_grad, early_steps(held, 1, 2))
        )
        return (
            query_grad.astype(jnp.bfloat16),
            key_grad.reshape(LENGTH, local_width).astype(jnp.bfloat16),
            value_grad.reshape(LENGTH, local_width).astype(jnp.bfloat16),
            held,
        )

    query_grads, key_grads, value_grads, held = backward_seq(
        (queries, key_rows, value_rows, lengths[0], grad_context, log_totals[0]), held
    )
    early_own = jnp.concatenate(
        [part.reshape(part.shape[-2:]) for part in early_steps(held, 2, len(orders[0]))], axis=1
    )
    whole = jnp.stack(
        [
            out_bias_grad,
            down_bias_grad,
            gain_one_grad,
            shift_one_grad,
            gain_two_grad,
            shift_two_grad,
        ]
    )
    whole_size = whole.size
    whole, up_bias_grad, query_grads = lax.optimization_barrier(
        (whole, up_bias_grad, query_grads)
    )
    early_small = sum_small(
        jnp.concatenate([(whole + swap_core(whole)).reshape(-1), up_bias_grad]).reshape(-1, 128)
    ).reshape(-1)
    query_grads = query_grads.reshape(seq_count * LENGTH, local_width)
    key_grads = key_grads.reshape(seq_count * LENGTH, local_width)
    value_grads = value_grads.reshape(seq_count * LENGTH, local_width)
    qv_bias_grad = jnp.stack(
        [
            jnp.sum(query_grads.astype(jnp.float32), axis=0),
            jnp.sum(value_grads.astype(jnp.float32), axis=0),
        ]
    )
    qkv_grad_own = jnp.stack(
        [
            scatter_rows(contract_rows(gathered, grads), orders[p % turns])
            for p, grads in enumerate((query_grads, key_grads, value_grads))
        ]
    )
    input_grad = (
        grad_first
        + sum_own(
            contract_cols(query_grads, qkv_back[0])
            + contract_cols(key_grads, qkv_back[1])
            + contract_cols(value_grads, qkv_back[2])
        )
    ).astype(jnp.bfloat16)
    qv_bias_total = sum_small(qv_bias_grad)
    out_grad_own = early_own[:, :out_width].T
    up_grad_own = early_own[:, out_width : out_width + up_width]
    down_grad_own = early_own[:, out_width + up_width :].T
    (
        out_bias_total,
        down_bias_total,
        gain_one_total,
        shift_one_total,
        gain_two_total,
        shift_two_total,
    ) = early_small[:whole_size].reshape(whole.shape)
    up_bias_total = early_small[whole_size:]
    return (
        layer_output,
        input_grad,
        qkv_grad_own,
        qv_bias_total,
        out_grad_own,
        out_bias_total,
        up_grad_own,
        up_bias_total,
        down_grad_own,
        down_bias_total,
        gain_one_total,
        shift_one_total,
        gain_two_total,
        shift_two_total,
    )


def solution(mesh):
    return jax.shard_map(
        per_device,
        mesh=mesh,
        in_specs=(
            P(("dp", "tensor"), None),
            P("dp"),
            P(None, "dp", "tensor"),
            P(None, "tensor"),
            P("tensor", "dp"),
            P(),
            P("dp", "tensor"),
            P("tensor"),
            P("tensor", "dp"),
            P(),
            P(),
            P(),
            P(),
            P(),
            P(("dp", "tensor"), None),
        ),
        out_specs=(
            P(("dp", "tensor"), None),
            P(("dp", "tensor"), None),
            P(None, "dp", "tensor"),
            P(None, "tensor"),
            P("tensor", "dp"),
            P(),
            P("dp", "tensor"),
            P("tensor"),
            P("tensor", "dp"),
            P(),
            P(),
            P(),
            P(),
            P(),
        ),
        check_vma=False,
    )
```
